32 devices in a mesh: parts: 2 (over y), dp: 4 (over z), tensor: 4 (over x, core).
Axes of the slice: x: 2, y: 2, z: 4, core: 2. Of those that a mesh axis runs over, the one named last changes fastest.
Arguments:
- tokens: bfloat16 [4096, 8192], P(('parts', 'dp'), 'tensor'), parts along dimension 0, may hold values from -6 to 6
- value_weight: bfloat16 [8192, 1024], P('tensor'), may hold values from -0.0625 to 0.0625
- down_panels: bfloat16 [12, 64, 8192], P('dp', None, 'tensor'), may hold values from -0.0625 to 0.0625
- up_panels: bfloat16 [12, 64, 1024], P('dp', None, 'tensor'), may hold values from -0.75 to 0.75
- adapter_rank: int32 [12], replicated, may hold values from 1 to 4
- adapter_slot: int32 [24], P('parts'), parts along dimension 0, may hold values from 0 to 11, as said below
- seg_adapter: int32 [8, 32], P(('parts', 'dp')), parts along dimension 0, may hold values from 0 to 11, as said below
- seg_lengths: int32 [8, 32], P(('parts', 'dp')), parts along dimension 0, may hold values from 1 to 64, 512 in all within a row
Outputs:
- projected: bfloat16 [4096, 1024], P(('parts', 'dp'), 'tensor'), parts along dimension 0
The draws below stay inside these ranges and needn't reach their ends.
There are 2 independent parts, one for each index of `parts`. The reference program is written for one: setup_inputs(seed, part) draws one part's arguments, and reference() takes and returns one part's arrays. A program takes and returns all parts, laid end to end along the dimension named above; an argument that names none is the same for every part. Nothing has to cross between parts.
Inputs may be any that keep to these rules, and one draw needn't show every extreme that they name: A permutation: adapter a is stored in row adapter_slot[a] of the panels, that is on dp index adapter_slot[a] // 3. `seg_adapter`: the requests of one replica name adapters stored on any one dp index at most 16 times, and exactly 16 times for some dp index in every replica. `seg_lengths`: each row sums to 512.
All inputs are finite; a program needn't handle non-finite values.
Results may differ from the reference program's by a relative error of at most 0.013.
Values may be sent and summed in bfloat16 or wider, within the bound.
A program may use at most 128 MiB of HBM per device.

```python
import math
import jax
import jax.numpy as jnp
import numpy as np
from jax import lax

D = 8192
VALUE_FEATURES = 1024
R = 64
TOK_DEV = 512
ADP_DEV = 3
REQUEST_COUNT = 32
LONGEST_TOKENS = 64
ADAPTERS = 12
TOTAL_TOKENS = 2048
CAP = 16
N_DP = 4
N_TENSOR = 4


def layout(key):
    slot = jax.random.permutation(jax.random.fold_in(key, 101), ADAPTERS).astype(jnp.int32)
    width = N_DP * CAP
    scores = jax.random.randint(jax.random.fold_in(key, 102), (N_DP, width), 0, 1 << 20)
    hottest = jax.random.randint(jax.random.fold_in(key, 103), (N_DP, 1), 0, N_DP)
    column = jnp.arange(width, dtype=jnp.int32)[None, :]
    scores = jnp.where(column // CAP == hottest, -1, scores)
    order = jnp.argsort(scores * width + column, axis=1)
    chosen = order[:, :REQUEST_COUNT]
    mixing = jax.random.randint(jax.random.fold_in(key, 104), (N_DP, REQUEST_COUNT), 0, 1 << 20)
    shuffle = jnp.argsort(mixing * REQUEST_COUNT + jnp.arange(REQUEST_COUNT, dtype=jnp.int32)[None, :], axis=1)
    chosen = jnp.take_along_axis(chosen, shuffle, axis=1)
    owner = chosen // CAP
    first_token = jax.random.randint(jax.random.fold_in(key, 105), (N_DP, REQUEST_COUNT), 0, ADP_DEV)
    second = jax.random.randint(jax.random.fold_in(key, 106), (N_DP, REQUEST_COUNT), 0, ADP_DEV)
    local = jnp.minimum(first_token, second)
    inverse = jnp.argsort(slot)
    named = inverse[owner * ADP_DEV + local]
    return (slot, named.astype(jnp.int32))


def draw_adapter_slot(key, part):
    slot, named = layout(key)
    return slot


def draw_seg_adapter(key, part):
    slot, named = layout(key)
    return named


def touch_ends(result, rng, smallest, largest):
    place = [jax.random.randint(jax.random.fold_in(rng, axis), (), 0, length) for axis, length in enumerate(result.shape)]
    main_axis = result.shape.index(max(result.shape))
    beside = place[:main_axis] + [(place[main_axis] + 1) % result.shape[main_axis]] + place[main_axis + 1:]
    return result.at[tuple(place)].set(smallest).at[tuple(beside)].set(largest)


def level_of(rng, shape, pieces, low, high):
    def one(dim, shards_of):
        heights = jax.random.uniform(jax.random.fold_in(jax.random.fold_in(rng, 6), dim), (shards_of,), jnp.float32, low / len(pieces), high / len(pieces))
        return jnp.repeat(jnp.exp(heights), shape[dim] // shards_of).reshape((-1,) + (1,) * (len(shape) - dim - 1))

    level = one(*pieces[0])
    for cut in pieces[1:]:
        level = level * one(*cut)
    return level


def profile(count, total, reach, slope):
    portions = [(1 << 20) // math.isqrt(standing ** slope) + 1 for standing in range(2, count + 1)]
    spare, holding = total - reach - (count - 1), [1] * (count - 1)
    while spare > 0:
        movable = [i for i in range(count - 1) if holding[i] < reach]
        pool, remaining = sum([portions[i] for i in movable]), spare
        for i in movable:
            addition = min(reach - holding[i], max(1, remaining * portions[i] // pool), spare)
            holding[i] = holding[i] + addition
            spare = spare - addition
    return np.array([reach] + holding)


def ragged_sizes(key, number_of, total, reach, slope):
    if number_of == 2:
        one = jax.random.randint(key, (), max(1, total - reach), min(reach, total - 1) + 1)
        return jnp.stack([one, total - one])
    lengths = jnp.asarray(profile(number_of, total, reach, slope), jnp.int32)
    twos = (number_of - 1) // 2
    giver, receiver = lengths[1:1 + 2 * twos:2], lengths[2:2 + 2 * twos:2]
    room = jnp.minimum(giver - 1, reach - receiver)
    shifted = jax.random.randint(jax.random.fold_in(key, 1), (twos,), 0, 1 << 20) % (room + 1)
    lengths = lengths.at[1:1 + 2 * twos:2].set(giver - shifted).at[2:2 + 2 * twos:2].set(receiver + shifted)
    return lengths[jax.random.permutation(jax.random.fold_in(key, 2), number_of)]


def bell_draw(rng, extent, scale, bound, cuts=(), held_as=jnp.bfloat16):
    gain = level_of(rng, extent, cuts, -0.22, 0.18) if cuts else 1.0
    result = jax.random.normal(rng, extent, jnp.float32) * scale * gain
    return jnp.minimum(jnp.maximum(result, -bound), bound).astype(held_as)


def setup_inputs(seed: int = 0, part: int = 0) -> dict:
    seeds = jax.random.split(jax.random.key(seed), 9)
    own_keys = jax.random.split(jax.random.fold_in(seeds[8], part), 9)
    tokens = bell_draw(own_keys[0], (TOTAL_TOKENS, D), 1.0, 6.0, ((0, 4), (1, 4)))
    value_weight = bell_draw(seeds[1], (D, VALUE_FEATURES), D ** -0.5, 0.0625, ((0, 4),))
    down_panels = bell_draw(seeds[2], (ADAPTERS, R, D), D ** -0.5, 0.0625, ((0, 4), (2, 4)))
    up_panels = bell_draw(seeds[3], (ADAPTERS, R, VALUE_FEATURES), R ** -0.5, 0.75, ((0, 4), (2, 4)))
    adapter_rank = touch_ends(jax.random.randint(seeds[4], (ADAPTERS,), 1, 5), jax.random.fold_in(seeds[4], 1), 1, 4).astype(jnp.int32)
    adapter_slot = draw_adapter_slot(jax.random.fold_in(jax.random.fold_in(seeds[8], part), 71), part)
    seg_adapter = draw_seg_adapter(jax.random.fold_in(jax.random.fold_in(seeds[8], part), 71), part)
    seg_lengths = jax.vmap(lambda own: ragged_sizes(own, REQUEST_COUNT, TOK_DEV, LONGEST_TOKENS, 2))(jax.random.split(own_keys[7], N_DP)).reshape((N_DP, REQUEST_COUNT)).astype(jnp.int32)
    return dict(tokens=tokens, value_weight=value_weight, down_panels=down_panels, up_panels=up_panels, adapter_rank=adapter_rank, adapter_slot=adapter_slot, seg_adapter=seg_adapter, seg_lengths=seg_lengths)


def reference(tokens, value_weight, down_panels, up_panels, adapter_rank, adapter_slot, seg_adapter, seg_lengths):
    block = D // N_TENSOR
    base_output = jnp.zeros((TOTAL_TOKENS, VALUE_FEATURES), jnp.float32)
    for part_index in range(N_TENSOR):
        term = jnp.dot(tokens[:, part_index * block:(part_index + 1) * block],
                       value_weight[part_index * block:(part_index + 1) * block],
                       preferred_element_type=jnp.float32)
        rounded = lax.optimization_barrier(term.astype(jnp.bfloat16))
        base_output = base_output + rounded.astype(jnp.float32)
    local_start = jnp.cumsum(seg_lengths, axis=1) - seg_lengths
    offsets = (jnp.arange(N_DP, dtype=jnp.int32) * TOK_DEV)[:, None]
    begin_flat = (local_start + offsets).reshape(-1).astype(jnp.int32)
    window_flat = (jnp.minimum(local_start, TOK_DEV - LONGEST_TOKENS) + offsets).reshape(-1).astype(jnp.int32)
    length_flat = seg_lengths.reshape(-1).astype(jnp.int32)
    rows_flat = adapter_slot[seg_adapter].reshape(-1).astype(jnp.int32)
    ranks_flat = (adapter_rank[rows_flat] * 16).astype(jnp.int32)
    segment_anchor = jnp.zeros((), jnp.int32)

    def visit_request(token_index, adapter_output):
        first_token = window_flat[token_index].astype(jnp.int32)
        row = rows_flat[token_index]
        piece = lax.dynamic_slice(tokens, (first_token, segment_anchor), (LONGEST_TOKENS, D))
        shrink = jnp.dot(piece, down_panels[row].T, preferred_element_type=jnp.float32)
        position = first_token + jnp.arange(LONGEST_TOKENS, dtype=jnp.int32)
        inside = (position >= begin_flat[token_index]) & (position < begin_flat[token_index] + length_flat[token_index])
        keep = jnp.arange(R, dtype=jnp.int32) < ranks_flat[token_index]
        shrink = jnp.where(inside[:, None] & keep[None, :], shrink, jnp.zeros_like(shrink))
        narrow = shrink.astype(jnp.bfloat16)
        adapter_update = jnp.dot(narrow, up_panels[row], preferred_element_type=jnp.float32)
        adapter_update = adapter_update * (32.0 / ranks_flat[token_index].astype(jnp.float32))
        current_request = lax.dynamic_slice(adapter_output, (first_token, segment_anchor), (LONGEST_TOKENS, VALUE_FEATURES))
        return lax.dynamic_update_slice(adapter_output, current_request + adapter_update, (first_token, segment_anchor))

    adapter_output = lax.fori_loop(0, N_DP * REQUEST_COUNT, visit_request, jnp.zeros((TOTAL_TOKENS, VALUE_FEATURES), jnp.float32))
    return (base_output + adapter_output).astype(jnp.bfloat16)
```

```python
import jax
import jax.numpy as jnp
from jax import lax
from jax.sharding import PartitionSpec as P


def local(
    tokens,
    value_weight,
    down_panels,
    up_panels,
    adapter_rank,
    adapter_slot,
    seg_adapter,
    seg_lengths,
):
    token_count, share = tokens.shape
    rank_pad = down_panels.shape[1]
    feature_share = up_panels.shape[2]
    adapters = adapter_rank.shape[0]
    lengths = seg_lengths[0]
    named = seg_adapter[0]
    down_all = lax.all_gather(down_panels, "dp", axis=0, tiled=True)
    up_all = lax.all_gather(up_panels, "dp", axis=0, tiled=True)
    partial_values = jnp.dot(tokens, value_weight, preferred_element_type=jnp.float32)
    base_output = lax.psum_scatter(
        partial_values.astype(jnp.bfloat16), "tensor", scatter_dimension=1, tiled=True
    ).astype(jnp.float32)
    ends = jnp.cumsum(lengths)
    position = jnp.arange(token_count, dtype=jnp.int32)[:, None]
    in_request = (position >= (ends - lengths)[None, :]) & (position < ends[None, :])
    storage_row = adapter_slot[named]
    token_row = jnp.sum(jnp.where(in_request, storage_row[None, :], 0), axis=1)
    column = jnp.arange(adapters * rank_pad, dtype=jnp.int32)
    column_row = column // rank_pad
    column_keep = column % rank_pad < 16 * adapter_rank[column_row]
    mask = (token_row[:, None] == column_row[None, :]) & column_keep[None, :]
    wide = lax.dot_general(
        tokens,
        down_all.reshape(adapters * rank_pad, share),
        (((1,), (1,)), ((), ())),
        preferred_element_type=jnp.float32,
    )
    shrink = jnp.where(mask, wide, 0.0).reshape(token_count, adapters, rank_pad).sum(axis=1)
    summed = lax.psum(shrink.astype(jnp.bfloat16), "tensor")
    spread = jnp.where(mask, jnp.tile(summed, (1, adapters)), 0)
    update = jnp.dot(
        spread, up_all.reshape(adapters * rank_pad, feature_share), preferred_element_type=jnp.float32
    )
    token_rank = (16 * adapter_rank[token_row]).astype(jnp.float32)
    return (base_output + update * (32.0 / token_rank)[:, None]).astype(jnp.bfloat16)


def solution(mesh):
    return jax.shard_map(
        local,
        mesh=mesh,
        in_specs=(
            P(("parts", "dp"), "tensor"),
            P("tensor", None),
            P("dp", None, "tensor"),
            P("dp", None, "tensor"),
            P(),
            P("parts"),
            P(("parts", "dp"), None),
            P(("parts", "dp"), None),
        ),
        out_specs=P(("parts", "dp"), "tensor"),
        check_vma=False,
    )
```

```python
import functools

import jax
import jax.numpy as jnp
from jax import lax
from jax.experimental import pallas as pl
from jax.experimental.pallas import tpu as pltpu
from jax.sharding import PartitionSpec as P

MESH = pl.DeviceIdType.MESH
BF16 = jnp.bfloat16
F32 = jnp.float32


def kernel(
    n, width, rank_pad, adapters_here, chunks,
    tokens_hbm, weight_hbm, down_hbm, up_hbm, rank_ref, slot_ref, named_ref, lengths_ref,
    out_ref,
    tokens, weight, down, up, code, wide_sum, base, value_send, value_recv, shrink_send, shrink_recv,
    local_sem, right_sem, left_sem, line_sem, pair_send, pair_recv,
    value_ssem, value_rsem, shrink_ssem, shrink_rsem,
):
    part, me, mine = lax.axis_index("parts"), lax.axis_index("dp"), lax.axis_index("tensor")
    token_count = tokens.shape[0]
    unit = adapters_here * rank_pad
    half = unit // 2
    piece = half // chunks
    share = up.shape[2]
    has_left, has_right = me > 0, me < n - 1

    copies = [
        pltpu.make_async_copy(tokens_hbm, tokens, local_sem.at[0]),
        pltpu.make_async_copy(weight_hbm, weight, local_sem.at[1]),
        pltpu.make_async_copy(down_hbm, down.at[me], local_sem.at[2]),
        pltpu.make_async_copy(up_hbm, up.at[me], local_sem.at[3]),
    ]
    for copy in copies:
        copy.start()

    barrier = pltpu.get_barrier_semaphore()

    def greet(where):
        pl.semaphore_signal(barrier, inc=1, device_id=where, device_id_type=MESH)

    @pl.when(has_left)
    def _():
        greet((part, me - 1, mine))

    @pl.when(has_right)
    def _():
        greet((part, me + 1, mine))

    greet((1 - part, me, mine))
    for i in range(1, width):
        greet((part, me, lax.rem(mine + i, width)))

    inner = has_left & has_right

    @pl.when(inner)
    def _():
        pl.semaphore_wait(barrier, width + 2)

    @pl.when(jnp.logical_not(inner))
    def _():
        pl.semaphore_wait(barrier, width + 1)

    def rows_of(which, c):
        if c == chunks:
            return pl.ds(pl.multiple_of(which * half, half), half)
        return pl.ds(pl.multiple_of(which * half + c * piece, piece), piece)

    def place(u, which, c):
        return (up if c == chunks else down).at[u, rows_of(which, c)]

    def line(u, c, to, sems, own=False):
        source = (up_hbm if c == chunks else down_hbm).at[rows_of(part, c)] if own else place(u, part, c)
        return pltpu.make_async_remote_copy(
            src_ref=source, dst_ref=place(u, part, c), send_sem=sems.at[u, c],
            recv_sem=line_sem.at[u, c], device_id=(part, to, mine), device_id_type=MESH)

    def pair(u, c, which):
        return pltpu.make_async_remote_copy(
            src_ref=place(u, which, c), dst_ref=place(u, which, c), send_sem=pair_send.at[u, c],
            recv_sem=pair_recv.at[u, c], device_id=(1 - part, me, mine), device_id_type=MESH)

    for c in range(chunks + 1):
        @pl.when(has_right)
        def _():
            line(me, c, me + 1, right_sem, own=True).start()

        @pl.when(has_left)
        def _():
            line(me, c, me - 1, left_sem, own=True).start()

    copies[0].wait()
    copies[1].wait()

    def value_copy(peer):
        return pltpu.make_async_remote_copy(
            src_ref=value_send.at[peer], dst_ref=value_recv.at[mine], send_sem=value_ssem.at[peer],
            recv_sem=value_rsem.at[mine], device_id=(part, me, peer), device_id_type=MESH)

    def value_arrival(peer):
        return pltpu.make_async_remote_copy(
            src_ref=value_send.at[peer], dst_ref=value_recv.at[peer], send_sem=value_ssem.at[peer],
            recv_sem=value_rsem.at[peer], device_id=(part, me, peer), device_id_type=MESH)

    def block_product(owner):
        columns = pl.ds(pl.multiple_of(owner * share, share), share)
        return jnp.dot(tokens[...], weight[:, columns], preferred_element_type=F32).astype(BF16)

    @pl.loop(1, width)
    def _(i):
        peer = lax.rem(mine + i, width)
        value_send[peer] = block_product(peer)
        value_copy(peer).start()

    base[...] = block_product(mine).astype(F32)

    position = lax.broadcasted_iota(jnp.int32, (token_count, unit), 0)

    def visit(j, carry):
        start, values = carry
        row = slot_ref[named_ref[0, j]]
        mark = row * 8 + rank_ref[row]
        return start + lengths_ref[0, j], jnp.where(position >= start, mark, values)

    code[...] = lax.fori_loop(
        0, lengths_ref.shape[1], visit, (jnp.int32(0), jnp.zeros((token_count, unit), jnp.int32)))[1]

    column = lax.broadcasted_iota(jnp.int32, (token_count, unit), 1) // rank_pad

    def at_unit(u):
        return (code[...] >> 3) == column + u * adapters_here

    def unit_shrink(u):
        product = lax.dot_general(
            tokens[...], down[u], (((1,), (1,)), ((), ())), preferred_element_type=F32)
        return jnp.where(at_unit(u), product, 0.0)

    copies[2].wait()
    wide_sum[...] = unit_shrink(me)

    def sides(step):
        return ((me - step, me - 1, me + 1, me - step >= 0, has_right, right_sem),
                (me + step, me + 1, me - 1, me + step < n, has_left, left_sem))

    def pass_on(step):
        for c in range(chunks + 1):
            for u, source, onward, there, more, sems in sides(step):
                @pl.when(there)
                def _():
                    line(u, c, source, sems).wait_recv()

                    @pl.when(more)
                    def _():
                        line(u, c, onward, sems).start()

                    pair(u, c, part).start()

    def take(step):
        for u, source, onward, there, more, sems in sides(step):
            @pl.when(there)
            def _():
                for c in range(chunks):
                    pair(u, c, 1 - part).wait_recv()
                wide_sum[...] += unit_shrink(u)

    pass_on(1)

    @pl.loop(2, n)
    def _(step):
        pass_on(step)
        take(step - 1)

    @pl.loop(1, width)
    def _(i):
        peer = lax.rem(mine + i, width)
        value_arrival(peer).wait_recv()
        base[...] += value_recv[peer].astype(F32)

    take(n - 1)

    def selector(height, test):
        i = lax.broadcasted_iota(jnp.int32, (height, 2 * rank_pad), 0)
        j = lax.broadcasted_iota(jnp.int32, (height, 2 * rank_pad), 1)
        return jnp.where(test(i, j), 1.0, 0.0).astype(BF16)

    fold = selector(unit, lambda i, j: i % rank_pad == j % rank_pad)
    twice = jnp.dot(wide_sum[...].astype(BF16), fold, preferred_element_type=F32)
    middle = token_count // 2
    lane = lax.broadcasted_iota(jnp.int32, (middle, 2 * rank_pad), 1)
    packed = jnp.where(lane < rank_pad, twice[:middle], twice[middle:])
    shrink_send[...] = packed.astype(BF16)

    def shrink_copy(peer, slot):
        return pltpu.make_async_remote_copy(
            src_ref=shrink_send, dst_ref=shrink_recv.at[slot], send_sem=shrink_ssem.at[peer],
            recv_sem=shrink_rsem.at[slot], device_id=(part, me, peer), device_id_type=MESH)

    for i in range(1, width):
        shrink_copy(lax.rem(mine + i, width), mine).start()
    total = shrink_send[...].astype(F32)
    for i in range(1, width):
        peer = lax.rem(mine + i, width)
        shrink_copy(peer, peer).wait_recv()
        total = total + shrink_recv[peer].astype(F32)
    narrow = total.astype(BF16)
    first = selector(2 * rank_pad, lambda i, j: i == j % rank_pad)
    second = selector(2 * rank_pad, lambda i, j: i == j % rank_pad + rank_pad)
    spread = jnp.concatenate(
        [jnp.dot(narrow, first, preferred_element_type=F32),
         jnp.dot(narrow, second, preferred_element_type=F32)], axis=0)
    lane = lax.broadcasted_iota(jnp.int32, (token_count, 2 * rank_pad), 1) % rank_pad
    spread = jnp.where(lane < 16 * (code[:, : 2 * rank_pad] & 7), spread, 0.0)
    copies_of = -(-unit // (2 * rank_pad))
    tiled = jnp.concatenate([spread] * copies_of, axis=1)[:, :unit]

    copies[3].wait()

    def lift(u, total):
        @pl.when(u != me)
        def _():
            pair(u, chunks, 1 - part).wait_recv()
        chosen = jnp.where(at_unit(u), tiled, 0.0).astype(BF16)
        return total + jnp.dot(chosen, up[u], preferred_element_type=F32)

    update = lax.fori_loop(0, n, lift, jnp.zeros((token_count, share), F32))
    scale = 32.0 / (16 * (code[:, :1] & 7)).astype(F32)
    out_ref[...] = (base[...] + update * scale).astype(BF16)

    @pl.loop(0, n)
    def _(u):
        for c in range(chunks + 1):
            @pl.when((u <= me) & has_right)
            def _():
                line(u, c, me + 1, right_sem).wait_send()

            @pl.when((u >= me) & has_left)
            def _():
                line(u, c, me - 1, left_sem).wait_send()

            @pl.when(u != me)
            def _():
                pair(u, c, part).wait_send()

    for i in range(1, width):
        peer = lax.rem(mine + i, width)
        value_copy(peer).wait_send()
        shrink_copy(peer, mine).wait_send()


def local(n, width, tokens, value_weight, down_panels, up_panels, adapter_rank, adapter_slot, seg_adapter, seg_lengths):
    token_count, depth = tokens.shape
    adapters_here, rank_pad, _ = down_panels.shape
    share = up_panels.shape[2]
    unit = adapters_here * rank_pad
    chunks = 3 if n <= 8 else 1
    dma = pltpu.SemaphoreType.DMA
    hbm = pl.BlockSpec(memory_space=pl.ANY)
    smem = pl.BlockSpec(memory_space=pltpu.SMEM)
    return pl.pallas_call(
        functools.partial(kernel, n, width, rank_pad, adapters_here, chunks),
        out_shape=jax.ShapeDtypeStruct((token_count, share), BF16),
        in_specs=[hbm] * 4 + [smem] * 4,
        out_specs=pl.BlockSpec(memory_space=pltpu.VMEM),
        scratch_shapes=[
            pltpu.VMEM(tokens.shape, BF16),
            pltpu.VMEM(value_weight.shape, BF16),
            pltpu.VMEM((n, unit, depth), BF16),
            pltpu.VMEM((n, unit, share), BF16),
            pltpu.VMEM((token_count, unit), jnp.int32),
            pltpu.VMEM((token_count, unit), F32),
            pltpu.VMEM((token_count, share), F32),
            pltpu.VMEM((width, token_count, share), BF16),
            pltpu.VMEM((width, token_count, share), BF16),
            pltpu.VMEM((token_count // 2, 2 * rank_pad), BF16),
            pltpu.VMEM((width, token_count // 2, 2 * rank_pad), BF16),
            dma((4,)),
            dma((n, chunks + 1)),
            dma((n, chunks + 1)),
            dma((n, chunks + 1)),
            dma((n, chunks + 1)),
            dma((n, chunks + 1)),
            dma((width,)),
            dma((width,)),
            dma((width,)),
            dma((width,)),
        ],
        compiler_params=pltpu.CompilerParams(
            collective_id=0, has_side_effects=True, vmem_limit_bytes=50 * 1024 * 1024),
    )(tokens, value_weight, down_panels.reshape(unit, depth), up_panels.reshape(unit, share),
      adapter_rank, adapter_slot, seg_adapter, seg_lengths)


def solution(mesh):
    return jax.shard_map(
        functools.partial(local, mesh.shape["dp"], mesh.shape["tensor"]),
        mesh=mesh,
        in_specs=(
            P(("parts", "dp"), "tensor"),
            P("tensor", None),
            P("dp", None, "tensor"),
            P("dp", None, "tensor"),
            P(),
            P("parts"),
            P(("parts", "dp"), None),
            P(("parts", "dp"), None),
        ),
        out_specs=P(("parts", "dp"), "tensor"),
        check_vma=False,
    )
```

```python
import functools

import jax
import jax.numpy as jnp
from jax import lax
from jax.experimental import pallas as pl
from jax.experimental.pallas import tpu as pltpu
from jax.sharding import PartitionSpec as P

MESH = pl.DeviceIdType.MESH
BF16 = jnp.bfloat16
F32 = jnp.float32


def kernel(
    n, width, rank_pad, adapters_here, chunks, window,
    tokens_hbm, weight_hbm, down_hbm, up_hbm, rank_hbm, slot_hbm, named_hbm, lengths_hbm,
    out_ref,
    rank_ref, slot_ref, named_ref, lengths_ref,
    tokens, weight, down, up, code, wide_sum, base, value_send, value_recv, shrink_send, shrink_recv,
    local_sem, right_sem, left_sem, line_sem, pair_send, pair_recv,
    value_ssem, value_rsem, shrink_ssem, shrink_rsem,
):
    part, me, mine = lax.axis_index("parts"), lax.axis_index("dp"), lax.axis_index("tensor")
    token_count = tokens.shape[0]
    unit = adapters_here * rank_pad
    half = unit // 2
    piece = half // chunks
    share = up.shape[2]
    has_left, has_right = me > 0, me < n - 1

    copies = [
        pltpu.make_async_copy(tokens_hbm, tokens, local_sem.at[0]),
        pltpu.make_async_copy(weight_hbm, weight, local_sem.at[1]),
        pltpu.make_async_copy(down_hbm, down.at[me], local_sem.at[2]),
        pltpu.make_async_copy(up_hbm, up.at[me], local_sem.at[3]),
        pltpu.make_async_copy(rank_hbm, rank_ref, local_sem.at[4]),
        pltpu.make_async_copy(slot_hbm, slot_ref, local_sem.at[5]),
        pltpu.make_async_copy(named_hbm, named_ref, local_sem.at[6]),
        pltpu.make_async_copy(lengths_hbm, lengths_ref, local_sem.at[7]),
    ]
    for copy in copies:
        copy.start()

    barrier = pltpu.get_barrier_semaphore()

    def greet(where):
        pl.semaphore_signal(barrier, inc=1, device_id=where, device_id_type=MESH)

    @pl.when(has_left)
    def _():
        greet((part, me - 1, mine))

    @pl.when(has_right)
    def _():
        greet((part, me + 1, mine))

    greet((1 - part, me, mine))
    for i in range(1, width):
        greet((part, me, lax.rem(mine + i, width)))

    inner = has_left & has_right

    @pl.when(inner)
    def _():
        pl.semaphore_wait(barrier, width + 2)

    @pl.when(jnp.logical_not(inner))
    def _():
        pl.semaphore_wait(barrier, width + 1)

    def rows_of(which, c):
        if c == chunks:
            return pl.ds(pl.multiple_of(which * half, half), half)
        return pl.ds(pl.multiple_of(which * half + c * piece, piece), piece)

    def place(u, which, c):
        return (up if c == chunks else down).at[u, rows_of(which, c)]

    def line(u, c, to, sems, own=False):
        source = (up_hbm if c == chunks else down_hbm).at[rows_of(part, c)] if own else place(u, part, c)
        return pltpu.make_async_remote_copy(
            src_ref=source, dst_ref=place(u, part, c), send_sem=sems.at[u, c],
            recv_sem=line_sem.at[u, c], device_id=(part, to, mine), device_id_type=MESH)

    def pair(u, c, which):
        return pltpu.make_async_remote_copy(
            src_ref=place(u, which, c), dst_ref=place(u, which, c), send_sem=pair_send.at[u, c],
            recv_sem=pair_recv.at[u, c], device_id=(1 - part, me, mine), device_id_type=MESH)

    def send_own(c):
        for to, there, sems in ((me + 1, has_right, right_sem), (me - 1, has_left, left_sem)):
            @pl.when(there)
            def _():
                if window <= c < chunks:
                    line(me, c - window, to, sems).wait_send()
                line(me, c, to, sems, own=True).start()

    for c in range(min(window, chunks)):
        send_own(c)

    copies[0].wait()
    copies[1].wait()

    def value_copy(peer):
        return pltpu.make_async_remote_copy(
            src_ref=value_send.at[peer], dst_ref=value_recv.at[mine], send_sem=value_ssem.at[peer],
            recv_sem=value_rsem.at[mine], device_id=(part, me, peer), device_id_type=MESH)

    def value_arrival(peer):
        return pltpu.make_async_remote_copy(
            src_ref=value_send.at[peer], dst_ref=value_recv.at[peer], send_sem=value_ssem.at[peer],
            recv_sem=value_rsem.at[peer], device_id=(part, me, peer), device_id_type=MESH)

    def block_product(owner):
        columns = pl.ds(pl.multiple_of(owner * share, share), share)
        return jnp.dot(tokens[...], weight[:, columns], preferred_element_type=F32).astype(BF16)

    @pl.loop(1, width)
    def _(i):
        peer = lax.rem(mine + i, width)
        value_send[peer] = block_product(peer)
        value_copy(peer).start()

    for c in range(window, chunks):
        send_own(c)
    base[...] = block_product(mine).astype(F32)

    position = lax.broadcasted_iota(jnp.int32, (token_count, unit), 0)

    def visit(j, carry):
        start, values = carry
        row = slot_ref[named_ref[0, j]]
        mark = row * 8 + rank_ref[row]
        return start + lengths_ref[0, j], jnp.where(position >= start, mark, values)

    for copy in copies[4:]:
        copy.wait()
    code[...] = lax.fori_loop(
        0, lengths_ref.shape[1], visit, (jnp.int32(0), jnp.zeros((token_count, unit), jnp.int32)))[1]

    column = lax.broadcasted_iota(jnp.int32, (token_count, unit), 1) // rank_pad

    def at_unit(u):
        return (code[...] >> 3) == column + u * adapters_here

    def unit_shrink(u):
        product = lax.dot_general(
            tokens[...], down[u], (((1,), (1,)), ((), ())), preferred_element_type=F32)
        return jnp.where(at_unit(u), product, 0.0)

    copies[2].wait()
    wide_sum[...] = unit_shrink(me)

    def sides(step):
        return ((me - step, me - 1, me + 1, me - step >= 0, has_right, right_sem),
                (me + step, me + 1, me - 1, me + step < n, has_left, left_sem))

    def pass_on(step, pieces):
        for c in pieces:
            for u, source, onward, there, more, sems in sides(step):
                @pl.when(there)
                def _():
                    line(u, c, source, sems).wait_recv()

                    @pl.when(more)
                    def _():
                        if c < chunks:
                            before = u if c >= window else u + me - source
                            line(before, (c - window) % chunks, onward, sems).wait_send()
                        line(u, c, onward, sems).start()

                    pair(u, c, part).start()

    def take(step):
        for u, source, onward, there, more, sems in sides(step):
            @pl.when(there)
            def _():
                for c in range(chunks):
                    pair(u, c, 1 - part).wait_recv()
                wide_sum[...] += unit_shrink(u)

    pass_on(1, range(chunks))

    @pl.loop(2, n)
    def _(step):
        pass_on(step, range(chunks))
        take(step - 1)

    @pl.loop(1, width)
    def _(i):
        peer = lax.rem(mine + i, width)
        value_arrival(peer).wait_recv()
        base[...] += value_recv[peer].astype(F32)

    take(n - 1)

    def selector(height, test):
        i = lax.broadcasted_iota(jnp.int32, (height, 2 * rank_pad), 0)
        j = lax.broadcasted_iota(jnp.int32, (height, 2 * rank_pad), 1)
        return jnp.where(test(i, j), 1.0, 0.0).astype(BF16)

    fold = selector(unit, lambda i, j: i % rank_pad == j % rank_pad)
    twice = jnp.dot(wide_sum[...].astype(BF16), fold, preferred_element_type=F32)
    middle = token_count // 2
    lane = lax.broadcasted_iota(jnp.int32, (middle, 2 * rank_pad), 1)
    packed = jnp.where(lane < rank_pad, twice[:middle], twice[middle:])
    shrink_send[...] = packed.astype(BF16)

    def shrink_copy(peer, slot):
        return pltpu.make_async_remote_copy(
            src_ref=shrink_send, dst_ref=shrink_recv.at[slot], send_sem=shrink_ssem.at[peer],
            recv_sem=shrink_rsem.at[slot], device_id=(part, me, peer), device_id_type=MESH)

    for i in range(1, width):
        shrink_copy(lax.rem(mine + i, width), mine).start()
    send_own(chunks)

    @pl.loop(1, n)
    def _(step):
        pass_on(step, [chunks])

    total = shrink_send[...].astype(F32)
    for i in range(1, width):
        peer = lax.rem(mine + i, width)
        shrink_copy(peer, peer).wait_recv()
        total = total + shrink_recv[peer].astype(F32)
    narrow = total.astype(BF16)
    first = selector(2 * rank_pad, lambda i, j: i == j % rank_pad)
    second = selector(2 * rank_pad, lambda i, j: i == j % rank_pad + rank_pad)
    spread = jnp.concatenate(
        [jnp.dot(narrow, first, preferred_element_type=F32),
         jnp.dot(narrow, second, preferred_element_type=F32)], axis=0)
    lane = lax.broadcasted_iota(jnp.int32, (token_count, 2 * rank_pad), 1) % rank_pad
    spread = jnp.where(lane < 16 * (code[:, : 2 * rank_pad] & 7), spread, 0.0)
    copies_of = -(-unit // (2 * rank_pad))
    tiled = jnp.concatenate([spread] * copies_of, axis=1)[:, :unit]

    copies[3].wait()

    def lift(u, total):
        @pl.when(u != me)
        def _():
            pair(u, chunks, 1 - part).wait_recv()
        chosen = jnp.where(at_unit(u), tiled, 0.0).astype(BF16)
        return total + jnp.dot(chosen, up[u], preferred_element_type=F32)

    update = lax.fori_loop(0, n, lift, jnp.zeros((token_count, share), F32))
    scale = 32.0 / (16 * (code[:, :1] & 7)).astype(F32)
    out_ref[...] = (base[...] + update * scale).astype(BF16)

    @pl.loop(0, n)
    def _(u):
        for c in range(chunks + 1):
            if c >= chunks - window:
                first = c == chunks

                @pl.when((u <= me if first else u == 0) & has_right)
                def _():
                    line(u, c, me + 1, right_sem).wait_send()

                @pl.when((u >= me if first else u == n - 1) & has_left)
                def _():
                    line(u, c, me - 1, left_sem).wait_send()

            @pl.when(u != me)
            def _():
                pair(u, c, part).wait_send()

    for i in range(1, width):
        peer = lax.rem(mine + i, width)
        value_copy(peer).wait_send()
        shrink_copy(peer, mine).wait_send()


def local(n, width, tokens, value_weight, down_panels, up_panels, adapter_rank, adapter_slot, seg_adapter, seg_lengths):
    token_count, depth = tokens.shape
    adapters_here, rank_pad, _ = down_panels.shape
    share = up_panels.shape[2]
    unit = adapters_here * rank_pad
    chunks, window = (3, 2) if n <= 8 else (1, 1)
    dma = pltpu.SemaphoreType.DMA
    hbm = pl.BlockSpec(memory_space=pltpu.HBM)
    return pl.pallas_call(
        functools.partial(kernel, n, width, rank_pad, adapters_here, chunks, window),
        out_shape=jax.ShapeDtypeStruct((token_count, share), BF16),
        in_specs=[hbm] * 8,
        out_specs=pl.BlockSpec(memory_space=pltpu.VMEM),
        scratch_shapes=[
            pltpu.SMEM(adapter_rank.shape, jnp.int32),
            pltpu.SMEM(adapter_slot.shape, jnp.int32),
            pltpu.SMEM(seg_adapter.shape, jnp.int32),
            pltpu.SMEM(seg_lengths.shape, jnp.int32),
            pltpu.VMEM(tokens.shape, BF16),
            pltpu.VMEM(value_weight.shape, BF16),
            pltpu.VMEM((n, unit, depth), BF16),
            pltpu.VMEM((n, unit, share), BF16),
            pltpu.VMEM((token_count, unit), jnp.int32),
            pltpu.VMEM((token_count, unit), F32),
            pltpu.VMEM((token_count, share), F32),
            pltpu.VMEM((width, token_count, share), BF16),
            pltpu.VMEM((width, token_count, share), BF16),
            pltpu.VMEM((token_count // 2, 2 * rank_pad), BF16),
            pltpu.VMEM((width, token_count // 2, 2 * rank_pad), BF16),
            dma((8,)),
            dma((n, chunks + 1)),
            dma((n, chunks + 1)),
            dma((n, chunks + 1)),
            dma((n, chunks + 1)),
            dma((n, chunks + 1)),
            dma((width,)),
            dma((width,)),
            dma((width,)),
            dma((width,)),
        ],
        compiler_params=pltpu.CompilerParams(
            collective_id=0, has_side_effects=True, vmem_limit_bytes=62 * 1024 * 1024),
    )(tokens, value_weight, down_panels.reshape(unit, depth), up_panels.reshape(unit, share),
      adapter_rank, adapter_slot, seg_adapter, seg_lengths)


def solution(mesh):
    return jax.shard_map(
        functools.partial(local, mesh.shape["dp"], mesh.shape["tensor"]),
        mesh=mesh,
        in_specs=(
            P(("parts", "dp"), "tensor"),
            P("tensor", None),
            P("dp", None, "tensor"),
            P("dp", None, "tensor"),
            P(),
            P("parts"),
            P(("parts", "dp"), None),
            P(("parts", "dp"), None),
        ),
        out_specs=P(("parts", "dp"), "tensor"),
        check_vma=False,
    )
```

```python
import functools

import jax
import jax.numpy as jnp
from jax import lax
from jax.experimental import pallas as pl
from jax.experimental.pallas import tpu as pltpu
from jax.sharding import PartitionSpec as P

MESH = pl.DeviceIdType.MESH
BF16 = jnp.bfloat16
F32 = jnp.float32


def kernel(
    n, width, rank_pad, adapters_here, chunks, window,
    tokens_hbm, weight_hbm, down_hbm, up_hbm, rank_hbm, slot_hbm, named_hbm, lengths_hbm,
    out_ref,
    rank_ref, slot_ref, named_ref, lengths_ref,
    tokens, weight, down, up, code, wide_sum, base, value_send, value_recv, shrink_send, shrink_recv,
    local_sem, right_sem, left_sem, line_sem, pair_send, pair_recv,
    value_ssem, value_rsem, shrink_ssem, shrink_rsem,
):
    part, me, mine = lax.axis_index("parts"), lax.axis_index("dp"), lax.axis_index("tensor")
    token_count = tokens.shape[0]
    unit = adapters_here * rank_pad
    half = unit // 2
    piece = half // chunks
    share = up.shape[2]
    has_left, has_right = me > 0, me < n - 1

    copies = [
        pltpu.make_async_copy(tokens_hbm, tokens, local_sem.at[0]),
        pltpu.make_async_copy(weight_hbm, weight, local_sem.at[1]),
        pltpu.make_async_copy(down_hbm, down.at[me], local_sem.at[2]),
        pltpu.make_async_copy(up_hbm, up.at[me], local_sem.at[3]),
        pltpu.make_async_copy(rank_hbm, rank_ref, local_sem.at[4]),
        pltpu.make_async_copy(slot_hbm, slot_ref, local_sem.at[5]),
        pltpu.make_async_copy(named_hbm, named_ref, local_sem.at[6]),
        pltpu.make_async_copy(lengths_hbm, lengths_ref, local_sem.at[7]),
    ]
    for copy in copies:
        copy.start()

    barrier = pltpu.get_barrier_semaphore()

    def greet(where):
        pl.semaphore_signal(barrier, inc=1, device_id=where, device_id_type=MESH)

    @pl.when(has_left)
    def _():
        greet((part, me - 1, mine))

    @pl.when(has_right)
    def _():
        greet((part, me + 1, mine))

    greet((1 - part, me, mine))
    for i in range(1, width):
        greet((part, me, lax.rem(mine + i, width)))

    inner = has_left & has_right

    @pl.when(inner)
    def _():
        pl.semaphore_wait(barrier, width + 2)

    @pl.when(jnp.logical_not(inner))
    def _():
        pl.semaphore_wait(barrier, width + 1)

    def rows_of(which, c):
        if c == chunks:
            return pl.ds(pl.multiple_of(which * half, half), half)
        return pl.ds(pl.multiple_of(which * half + c * piece, piece), piece)

    def place(u, which, c):
        return (up if c == chunks else down).at[u, rows_of(which, c)]

    def line(u, c, to, sems, own=False):
        source = (up_hbm if c == chunks else down_hbm).at[rows_of(part, c)] if own else place(u, part, c)
        return pltpu.make_async_remote_copy(
            src_ref=source, dst_ref=place(u, part, c), send_sem=sems.at[u, c],
            recv_sem=line_sem.at[u, c], device_id=(part, to, mine), device_id_type=MESH)

    def pair(u, c, which):
        return pltpu.make_async_remote_copy(
            src_ref=place(u, which, c), dst_ref=place(u, which, c), send_sem=pair_send.at[u, c],
            recv_sem=pair_recv.at[u, c], device_id=(1 - part, me, mine), device_id_type=MESH)

    def send_own(c):
        for to, there, sems in ((me + 1, has_right, right_sem), (me - 1, has_left, left_sem)):
            @pl.when(there)
            def _():
                if window and window <= c < chunks:
                    line(me, c - window, to, sems).wait_send()
                line(me, c, to, sems, own=True).start()

    first_pieces = min(window or chunks, chunks)
    for c in range(first_pieces):
        send_own(c)

    copies[0].wait()
    copies[1].wait()

    def value_copy(peer):
        return pltpu.make_async_remote_copy(
            src_ref=value_send.at[peer], dst_ref=value_recv.at[mine], send_sem=value_ssem.at[peer],
            recv_sem=value_rsem.at[mine], device_id=(part, me, peer), device_id_type=MESH)

    def value_arrival(peer):
        return pltpu.make_async_remote_copy(
            src_ref=value_send.at[peer], dst_ref=value_recv.at[peer], send_sem=value_ssem.at[peer],
            recv_sem=value_rsem.at[peer], device_id=(part, me, peer), device_id_type=MESH)

    def block_product(owner):
        columns = pl.ds(pl.multiple_of(owner * share, share), share)
        return jnp.dot(tokens[...], weight[:, columns], preferred_element_type=F32).astype(BF16)

    @pl.loop(1, width)
    def _(i):
        peer = lax.rem(mine + i, width)
        value_send[peer] = block_product(peer)
        value_copy(peer).start()

    for c in range(first_pieces, chunks):
        send_own(c)
    base[...] = block_product(mine).astype(F32)

    position = lax.broadcasted_iota(jnp.int32, (token_count, unit), 0)

    def visit(j, carry):
        start, values = carry
        row = slot_ref[named_ref[0, j]]
        mark = row * 8 + rank_ref[row]
        return start + lengths_ref[0, j], jnp.where(position >= start, mark, values)

    for copy in copies[4:]:
        copy.wait()
    code[...] = lax.fori_loop(
        0, lengths_ref.shape[1], visit, (jnp.int32(0), jnp.zeros((token_count, unit), jnp.int32)))[1]

    column = lax.broadcasted_iota(jnp.int32, (token_count, unit), 1) // rank_pad

    def at_unit(u):
        return (code[...] >> 3) == column + u * adapters_here

    def unit_shrink(u):
        product = lax.dot_general(
            tokens[...], down[u], (((1,), (1,)), ((), ())), preferred_element_type=F32)
        return jnp.where(at_unit(u), product, 0.0)

    copies[2].wait()
    wide_sum[...] = unit_shrink(me)

    def sides(step):
        return ((me - step, me - 1, me + 1, me - step >= 0, has_right, right_sem),
                (me + step, me + 1, me - 1, me + step < n, has_left, left_sem))

    def pass_on(step, pieces):
        for c in pieces:
            for u, source, onward, there, more, sems in sides(step):
                @pl.when(there)
                def _():
                    line(u, c, source, sems).wait_recv()

                    @pl.when(more)
                    def _():
                        if window and c < chunks:
                            before = u if c >= window else u + me - source
                            line(before, (c - window) % chunks, onward, sems).wait_send()
                        line(u, c, onward, sems).start()

                    pair(u, c, part).start()

    def take(step):
        for u, source, onward, there, more, sems in sides(step):
            @pl.when(there)
            def _():
                for c in range(chunks):
                    pair(u, c, 1 - part).wait_recv()
                wide_sum[...] += unit_shrink(u)

    pass_on(1, range(chunks))
    send_own(chunks)

    @pl.loop(2, n)
    def _(step):
        pass_on(step, range(chunks))
        pass_on(step - 1, [chunks])
        take(step - 1)

    @pl.loop(1, width)
    def _(i):
        peer = lax.rem(mine + i, width)
        value_arrival(peer).wait_recv()
        base[...] += value_recv[peer].astype(F32)

    take(n - 1)

    def selector(height, test):
        i = lax.broadcasted_iota(jnp.int32, (height, 2 * rank_pad), 0)
        j = lax.broadcasted_iota(jnp.int32, (height, 2 * rank_pad), 1)
        return jnp.where(test(i, j), 1.0, 0.0).astype(BF16)

    fold = selector(unit, lambda i, j: i % rank_pad == j % rank_pad)
    twice = jnp.dot(wide_sum[...].astype(BF16), fold, preferred_element_type=F32)
    middle = token_count // 2
    lane = lax.broadcasted_iota(jnp.int32, (middle, 2 * rank_pad), 1)
    packed = jnp.where(lane < rank_pad, twice[:middle], twice[middle:])
    shrink_send[...] = packed.astype(BF16)

    def shrink_copy(peer, slot):
        return pltpu.make_async_remote_copy(
            src_ref=shrink_send, dst_ref=shrink_recv.at[slot], send_sem=shrink_ssem.at[peer],
            recv_sem=shrink_rsem.at[slot], device_id=(part, me, peer), device_id_type=MESH)

    for i in range(1, width):
        shrink_copy(lax.rem(mine + i, width), mine).start()
    pass_on(n - 1, [chunks])
    total = shrink_send[...].astype(F32)
    for i in range(1, width):
        peer = lax.rem(mine + i, width)
        shrink_copy(peer, peer).wait_recv()
        total = total + shrink_recv[peer].astype(F32)
    narrow = total.astype(BF16)
    first = selector(2 * rank_pad, lambda i, j: i == j % rank_pad)
    second = selector(2 * rank_pad, lambda i, j: i == j % rank_pad + rank_pad)
    spread = jnp.concatenate(
        [jnp.dot(narrow, first, preferred_element_type=F32),
         jnp.dot(narrow, second, preferred_element_type=F32)], axis=0)
    lane = lax.broadcasted_iota(jnp.int32, (token_count, 2 * rank_pad), 1) % rank_pad
    spread = jnp.where(lane < 16 * (code[:, : 2 * rank_pad] & 7), spread, 0.0)
    copies_of = -(-unit // (2 * rank_pad))
    tiled = jnp.concatenate([spread] * copies_of, axis=1)[:, :unit]

    copies[3].wait()

    def lift(u, total):
        @pl.when(u != me)
        def _():
            pair(u, chunks, 1 - part).wait_recv()
        chosen = jnp.where(at_unit(u), tiled, 0.0).astype(BF16)
        return total + jnp.dot(chosen, up[u], preferred_element_type=F32)

    update = lax.fori_loop(0, n, lift, jnp.zeros((token_count, share), F32))
    scale = 32.0 / (16 * (code[:, :1] & 7)).astype(F32)
    out_ref[...] = (base[...] + update * scale).astype(BF16)

    @pl.loop(0, n)
    def _(u):
        for c in range(chunks + 1):
            if not window or c >= chunks - window:
                first = c == chunks or not window

                @pl.when((u <= me if first else u == 0) & has_right)
                def _():
                    line(u, c, me + 1, right_sem).wait_send()

                @pl.when((u >= me if first else u == n - 1) & has_left)
                def _():
                    line(u, c, me - 1, left_sem).wait_send()

            @pl.when(u != me)
            def _():
                pair(u, c, part).wait_send()

    for i in range(1, width):
        peer = lax.rem(mine + i, width)
        value_copy(peer).wait_send()
        shrink_copy(peer, mine).wait_send()


def local(n, width, tokens, value_weight, down_panels, up_panels, adapter_rank, adapter_slot, seg_adapter, seg_lengths):
    token_count, depth = tokens.shape
    adapters_here, rank_pad, _ = down_panels.shape
    share = up_panels.shape[2]
    unit = adapters_here * rank_pad
    chunks, window = (3, 0) if n <= 8 else (1, 0)
    dma = pltpu.SemaphoreType.DMA
    hbm = pl.BlockSpec(memory_space=pltpu.HBM)
    return pl.pallas_call(
        functools.partial(kernel, n, width, rank_pad, adapters_here, chunks, window),
        out_shape=jax.ShapeDtypeStruct((token_count, share), BF16),
        in_specs=[hbm] * 8,
        out_specs=pl.BlockSpec(memory_space=pltpu.VMEM),
        scratch_shapes=[
            pltpu.SMEM(adapter_rank.shape, jnp.int32),
            pltpu.SMEM(adapter_slot.shape, jnp.int32),
            pltpu.SMEM(seg_adapter.shape, jnp.int32),
            pltpu.SMEM(seg_lengths.shape, jnp.int32),
            pltpu.VMEM(tokens.shape, BF16),
            pltpu.VMEM(value_weight.shape, BF16),
            pltpu.VMEM((n, unit, depth), BF16),
            pltpu.VMEM((n, unit, share), BF16),
            pltpu.VMEM((token_count, unit), jnp.int32),
            pltpu.VMEM((token_count, unit), F32),
            pltpu.VMEM((token_count, share), F32),
            pltpu.VMEM((width, token_count, share), BF16),
            pltpu.VMEM((width, token_count, share), BF16),
            pltpu.VMEM((token_count // 2, 2 * rank_pad), BF16),
            pltpu.VMEM((width, token_count // 2, 2 * rank_pad), BF16),
            dma((8,)),
            dma((n, chunks + 1)),
            dma((n, chunks + 1)),
            dma((n, chunks + 1)),
            dma((n, chunks + 1)),
            dma((n, chunks + 1)),
            dma((width,)),
            dma((width,)),
            dma((width,)),
            dma((width,)),
        ],
        compiler_params=pltpu.CompilerParams(
            collective_id=0, has_side_effects=True, vmem_limit_bytes=62 * 1024 * 1024),
    )(tokens, value_weight, down_panels.reshape(unit, depth), up_panels.reshape(unit, share),
      adapter_rank, adapter_slot, seg_adapter, seg_lengths)


def solution(mesh):
    return jax.shard_map(
        functools.partial(local, mesh.shape["dp"], mesh.shape["tensor"]),
        mesh=mesh,
        in_specs=(
            P(("parts", "dp"), "tensor"),
            P("tensor", None),
            P("dp", None, "tensor"),
            P("dp", None, "tensor"),
            P(),
            P("parts"),
            P(("parts", "dp"), None),
            P(("parts", "dp"), None),
        ),
        out_specs=P(("parts", "dp"), "tensor"),
        check_vma=False,
    )
```

```python
import functools

import jax
import jax.numpy as jnp
from jax import lax
from jax.experimental import pallas as pl
from jax.experimental.pallas import tpu as pltpu
from jax.sharding import PartitionSpec as P

MESH = pl.DeviceIdType.MESH
BF16 = jnp.bfloat16
F32 = jnp.float32


def kernel(
    n, width, rank_pad, adapters_here, chunks, window,
    tokens_hbm, weight_hbm, down_hbm, up_hbm, rank_hbm, slot_hbm, named_hbm, lengths_hbm,
    out_ref,
    rank_ref, slot_ref, named_ref, lengths_ref,
    tokens, weight, down, up, code, wide_sum, base, value_send, value_recv, shrink_send, shrink_recv,
    local_sem, right_sem, left_sem, line_sem, pair_send, pair_recv,
    value_ssem, value_rsem, shrink_ssem, shrink_rsem,
):
    part, me, mine = lax.axis_index("parts"), lax.axis_index("dp"), lax.axis_index("tensor")
    token_count = tokens.shape[0]
    unit = adapters_here * rank_pad
    half = unit // 2
    piece = half // chunks
    share = up.shape[2]
    has_left, has_right = me > 0, me < n - 1

    copies = [
        pltpu.make_async_copy(tokens_hbm, tokens, local_sem.at[0]),
        pltpu.make_async_copy(weight_hbm, weight, local_sem.at[1]),
        pltpu.make_async_copy(down_hbm, down.at[me], local_sem.at[2]),
        pltpu.make_async_copy(up_hbm, up.at[me], local_sem.at[3]),
        pltpu.make_async_copy(rank_hbm, rank_ref, local_sem.at[4]),
        pltpu.make_async_copy(slot_hbm, slot_ref, local_sem.at[5]),
        pltpu.make_async_copy(named_hbm, named_ref, local_sem.at[6]),
        pltpu.make_async_copy(lengths_hbm, lengths_ref, local_sem.at[7]),
    ]
    for copy in copies:
        copy.start()

    barrier = pltpu.get_barrier_semaphore()

    def greet(where):
        pl.semaphore_signal(barrier, inc=1, device_id=where, device_id_type=MESH)

    @pl.when(has_left)
    def _():
        greet((part, me - 1, mine))

    @pl.when(has_right)
    def _():
        greet((part, me + 1, mine))

    greet((1 - part, me, mine))
    for i in range(1, width):
        greet((part, me, lax.rem(mine + i, width)))

    inner = has_left & has_right

    @pl.when(inner)
    def _():
        pl.semaphore_wait(barrier, width + 2)

    @pl.when(jnp.logical_not(inner))
    def _():
        pl.semaphore_wait(barrier, width + 1)

    def rows_of(which, c):
        if c == chunks + 1:
            which, c = 1 - which, chunks - 1
        if c == chunks:
            return pl.ds(pl.multiple_of(which * half, half), half)
        return pl.ds(pl.multiple_of(which * half + c * piece, piece), piece)

    def place(u, which, c):
        return (up if c == chunks else down).at[u, rows_of(which, c)]

    def line(u, c, to, sems, own=False):
        source = (up_hbm if c == chunks else down_hbm).at[rows_of(part, c)] if own else place(u, part, c)
        return pltpu.make_async_remote_copy(
            src_ref=source, dst_ref=place(u, part, c), send_sem=sems.at[u, c],
            recv_sem=line_sem.at[u, c], device_id=(part, to, mine), device_id_type=MESH)

    def pair(u, c, which):
        return pltpu.make_async_remote_copy(
            src_ref=place(u, which, c), dst_ref=place(u, which, c), send_sem=pair_send.at[u, c],
            recv_sem=pair_recv.at[u, c], device_id=(1 - part, me, mine), device_id_type=MESH)

    def send_own(c):
        for to, there, sems in ((me + 1, has_right, right_sem), (me - 1, has_left, left_sem)):
            @pl.when(there)
            def _():
                line(me, c, to, sems, own=True).start()

    first_pieces = min(window or chunks, chunks)
    for c in range(first_pieces):
        send_own(c)

    @pl.when((me == 0) | (me == n - 1))
    def _():
        send_own(chunks + 1)

    copies[0].wait()
    copies[1].wait()

    def value_copy(peer):
        return pltpu.make_async_remote_copy(
            src_ref=value_send.at[peer], dst_ref=value_recv.at[mine], send_sem=value_ssem.at[peer],
            recv_sem=value_rsem.at[mine], device_id=(part, me, peer), device_id_type=MESH)

    def value_arrival(peer):
        return pltpu.make_async_remote_copy(
            src_ref=value_send.at[peer], dst_ref=value_recv.at[peer], send_sem=value_ssem.at[peer],
            recv_sem=value_rsem.at[peer], device_id=(part, me, peer), device_id_type=MESH)

    def block_product(owner):
        columns = pl.ds(pl.multiple_of(owner * share, share), share)
        return jnp.dot(tokens[...], weight[:, columns], preferred_element_type=F32).astype(BF16)

    @pl.loop(1, width)
    def _(i):
        peer = lax.rem(mine + i, width)
        value_send[peer] = block_product(peer)
        value_copy(peer).start()

    for c in range(first_pieces, chunks):
        send_own(c)
    base[...] = block_product(mine).astype(F32)

    position = lax.broadcasted_iota(jnp.int32, (token_count, unit), 0)

    def visit(j, carry):
        start, values = carry
        row = slot_ref[named_ref[0, j]]
        mark = row * 8 + rank_ref[row]
        return start + lengths_ref[0, j], jnp.where(position >= start, mark, values)

    for copy in copies[4:]:
        copy.wait()
    code[...] = lax.fori_loop(
        0, lengths_ref.shape[1], visit, (jnp.int32(0), jnp.zeros((token_count, unit), jnp.int32)))[1]

    column = lax.broadcasted_iota(jnp.int32, (token_count, unit), 1) // rank_pad

    def at_unit(u):
        return (code[...] >> 3) == column + u * adapters_here

    def unit_shrink(u):
        product = lax.dot_general(
            tokens[...], down[u], (((1,), (1,)), ((), ())), preferred_element_type=F32)
        return jnp.where(at_unit(u), product, 0.0)

    copies[2].wait()
    wide_sum[...] = unit_shrink(me)

    def sides(step):
        return ((me - step, me - 1, me + 1, me - step >= 0, has_right, right_sem, me == step),
                (me + step, me + 1, me - 1, me + step < n, has_left, left_sem, me + step == n - 1))

    def pass_on(step, pieces):
        for c in pieces:
            for u, source, onward, there, more, sems, end in sides(step):
                @pl.when(there & end if c == chunks + 1 else there)
                def _():
                    line(u, c, source, sems).wait_recv()

                    @pl.when(more)
                    def _():
                        line(u, c, onward, sems).start()

                    if c == chunks - 1:
                        @pl.when(jnp.logical_not(end))
                        def _():
                            pair(u, c, part).start()
                    elif c <= chunks:
                        pair(u, c, part).start()

    def take(step):
        for u, source, onward, there, more, sems, end in sides(step):
            @pl.when(there)
            def _():
                for c in range(chunks - 1):
                    pair(u, c, 1 - part).wait_recv()

                @pl.when(jnp.logical_not(end))
                def _():
                    pair(u, chunks - 1, 1 - part).wait_recv()
                wide_sum[...] += unit_shrink(u)

    down_pieces = [*range(chunks), chunks + 1]
    pass_on(1, down_pieces)
    send_own(chunks)

    @pl.loop(2, n)
    def _(step):
        pass_on(step, down_pieces)
        pass_on(step - 1, [chunks])
        take(step - 1)

    @pl.loop(1, width)
    def _(i):
        peer = lax.rem(mine + i, width)
        value_arrival(peer).wait_recv()
        base[...] += value_recv[peer].astype(F32)

    take(n - 1)

    def selector(height, test):
        i = lax.broadcasted_iota(jnp.int32, (height, 2 * rank_pad), 0)
        j = lax.broadcasted_iota(jnp.int32, (height, 2 * rank_pad), 1)
        return jnp.where(test(i, j), 1.0, 0.0).astype(BF16)

    fold = selector(unit, lambda i, j: i % rank_pad == j % rank_pad)
    twice = jnp.dot(wide_sum[...].astype(BF16), fold, preferred_element_type=F32)
    middle = token_count // 2
    lane = lax.broadcasted_iota(jnp.int32, (middle, 2 * rank_pad), 1)
    packed = jnp.where(lane < rank_pad, twice[:middle], twice[middle:])
    shrink_send[...] = packed.astype(BF16)

    def shrink_copy(peer, slot):
        return pltpu.make_async_remote_copy(
            src_ref=shrink_send, dst_ref=shrink_recv.at[slot], send_sem=shrink_ssem.at[peer],
            recv_sem=shrink_rsem.at[slot], device_id=(part, me, peer), device_id_type=MESH)

    for i in range(1, width):
        shrink_copy(lax.rem(mine + i, width), mine).start()
    pass_on(n - 1, [chunks])
    total = shrink_send[...].astype(F32)
    for i in range(1, width):
        peer = lax.rem(mine + i, width)
        shrink_copy(peer, peer).wait_recv()
        total = total + shrink_recv[peer].astype(F32)
    narrow = total.astype(BF16)
    first = selector(2 * rank_pad, lambda i, j: i == j % rank_pad)
    second = selector(2 * rank_pad, lambda i, j: i == j % rank_pad + rank_pad)
    spread = jnp.concatenate(
        [jnp.dot(narrow, first, preferred_element_type=F32),
         jnp.dot(narrow, second, preferred_element_type=F32)], axis=0)
    lane = lax.broadcasted_iota(jnp.int32, (token_count, 2 * rank_pad), 1) % rank_pad
    spread = jnp.where(lane < 16 * (code[:, : 2 * rank_pad] & 7), spread, 0.0)
    copies_of = -(-unit // (2 * rank_pad))
    tiled = jnp.concatenate([spread] * copies_of, axis=1)[:, :unit]

    copies[3].wait()

    def lift(u, total):
        @pl.when(u != me)
        def _():
            pair(u, chunks, 1 - part).wait_recv()
        chosen = jnp.where(at_unit(u), tiled, 0.0).astype(BF16)
        return total + jnp.dot(chosen, up[u], preferred_element_type=F32)

    update = lax.fori_loop(0, n, lift, jnp.zeros((token_count, share), F32))
    scale = 32.0 / (16 * (code[:, :1] & 7)).astype(F32)
    out_ref[...] = (base[...] + update * scale).astype(BF16)

    @pl.loop(0, n)
    def _(u):
        for c in range(chunks + 1):
            if not window or c >= chunks - window:
                first = c == chunks or not window

                @pl.when((u <= me if first else u == 0) & has_right)
                def _():
                    line(u, c, me + 1, right_sem).wait_send()

                @pl.when((u >= me if first else u == n - 1) & has_left)
                def _():
                    line(u, c, me - 1, left_sem).wait_send()

            @pl.when((u != me) & (u != 0) & (u != n - 1) if c == chunks - 1 else u != me)
            def _():
                pair(u, c, part).wait_send()

    @pl.when(has_right)
    def _():
        line(0, chunks + 1, me + 1, right_sem).wait_send()

    @pl.when(has_left)
    def _():
        line(n - 1, chunks + 1, me - 1, left_sem).wait_send()

    for i in range(1, width):
        peer = lax.rem(mine + i, width)
        value_copy(peer).wait_send()
        shrink_copy(peer, mine).wait_send()


def local(n, width, tokens, value_weight, down_panels, up_panels, adapter_rank, adapter_slot, seg_adapter, seg_lengths):
    token_count, depth = tokens.shape
    adapters_here, rank_pad, _ = down_panels.shape
    share = up_panels.shape[2]
    unit = adapters_here * rank_pad
    chunks, window = (3, 0) if n <= 8 else (1, 0)
    dma = pltpu.SemaphoreType.DMA
    hbm = pl.BlockSpec(memory_space=pltpu.HBM)
    return pl.pallas_call(
        functools.partial(kernel, n, width, rank_pad, adapters_here, chunks, window),
        out_shape=jax.ShapeDtypeStruct((token_count, share), BF16),
        in_specs=[hbm] * 8,
        out_specs=pl.BlockSpec(memory_space=pltpu.VMEM),
        scratch_shapes=[
            pltpu.SMEM(adapter_rank.shape, jnp.int32),
            pltpu.SMEM(adapter_slot.shape, jnp.int32),
            pltpu.SMEM(seg_adapter.shape, jnp.int32),
            pltpu.SMEM(seg_lengths.shape, jnp.int32),
            pltpu.VMEM(tokens.shape, BF16),
            pltpu.VMEM(value_weight.shape, BF16),
            pltpu.VMEM((n, unit, depth), BF16),
            pltpu.VMEM((n, unit, share), BF16),
            pltpu.VMEM((token_count, unit), jnp.int32),
            pltpu.VMEM((token_count, unit), F32),
            pltpu.VMEM((token_count, share), F32),
            pltpu.VMEM((width, token_count, share), BF16),
            pltpu.VMEM((width, token_count, share), BF16),
            pltpu.VMEM((token_count // 2, 2 * rank_pad), BF16),
            pltpu.VMEM((width, token_count // 2, 2 * rank_pad), BF16),
            dma((8,)),
            dma((n, chunks + 2)),
            dma((n, chunks + 2)),
            dma((n, chunks + 2)),
            dma((n, chunks + 2)),
            dma((n, chunks + 2)),
            dma((width,)),
            dma((width,)),
            dma((width,)),
            dma((width,)),
        ],
        compiler_params=pltpu.CompilerParams(
            collective_id=0, has_side_effects=True, vmem_limit_bytes=62 * 1024 * 1024),
    )(tokens, value_weight, down_panels.reshape(unit, depth), up_panels.reshape(unit, share),
      adapter_rank, adapter_slot, seg_adapter, seg_lengths)


def solution(mesh):
    return jax.shard_map(
        functools.partial(local, mesh.shape["dp"], mesh.shape["tensor"]),
        mesh=mesh,
        in_specs=(
            P(("parts", "dp"), "tensor"),
            P("tensor", None),
            P("dp", None, "tensor"),
            P("dp", None, "tensor"),
            P(),
            P("parts"),
            P(("parts", "dp"), None),
            P(("parts", "dp"), None),
        ),
        out_specs=P(("parts", "dp"), "tensor"),
        check_vma=False,
    )
```

```python
import functools

import jax
import jax.numpy as jnp
from jax import lax
from jax.experimental import pallas as pl
from jax.experimental.pallas import tpu as pltpu
from jax.sharding import PartitionSpec as P

MESH = pl.DeviceIdType.MESH
BF16 = jnp.bfloat16
F32 = jnp.float32


def kernel(
    n, width, rank_pad, adapters_here, chunks, window,
    tokens_hbm, weight_hbm, down_hbm, up_hbm, rank_hbm, slot_hbm, named_hbm, lengths_hbm,
    out_ref,
    rank_ref, slot_ref, named_ref, lengths_ref,
    tokens, weight, down, up, code, wide_sum, base, value_send, value_recv, shrink_send, shrink_recv,
    local_sem, right_sem, left_sem, line_sem, pair_send, pair_recv,
    value_ssem, value_rsem, shrink_ssem, shrink_rsem,
):
    part, me, mine = lax.axis_index("parts"), lax.axis_index("dp"), lax.axis_index("tensor")
    token_count = tokens.shape[0]
    unit = adapters_here * rank_pad
    half = unit // 2
    piece = half // chunks
    share = up.shape[2]
    has_left, has_right = me > 0, me < n - 1

    copies = [
        pltpu.make_async_copy(tokens_hbm, tokens, local_sem.at[0]),
        pltpu.make_async_copy(weight_hbm, weight, local_sem.at[1]),
        pltpu.make_async_copy(down_hbm, down.at[me], local_sem.at[2]),
        pltpu.make_async_copy(up_hbm, up.at[me], local_sem.at[3]),
        pltpu.make_async_copy(rank_hbm, rank_ref, local_sem.at[4]),
        pltpu.make_async_copy(slot_hbm, slot_ref, local_sem.at[5]),
        pltpu.make_async_copy(named_hbm, named_ref, local_sem.at[6]),
        pltpu.make_async_copy(lengths_hbm, lengths_ref, local_sem.at[7]),
    ]
    for copy in copies:
        copy.start()

    barrier = pltpu.get_barrier_semaphore()

    def greet(where):
        pl.semaphore_signal(barrier, inc=1, device_id=where, device_id_type=MESH)

    @pl.when(has_left)
    def _():
        greet((part, me - 1, mine))

    @pl.when(has_right)
    def _():
        greet((part, me + 1, mine))

    greet((1 - part, me, mine))
    for i in range(1, width):
        greet((part, me, lax.rem(mine + i, width)))

    inner = has_left & has_right

    @pl.when(inner)
    def _():
        pl.semaphore_wait(barrier, width + 2)

    @pl.when(jnp.logical_not(inner))
    def _():
        pl.semaphore_wait(barrier, width + 1)

    def rows_of(which, c):
        if c == chunks + 1:
            which, c = 1 - which, chunks - 1
        if c == chunks:
            return pl.ds(pl.multiple_of(which * half, half), half)
        return pl.ds(pl.multiple_of(which * half + c * piece, piece), piece)

    def place(u, which, c):
        return (up if c == chunks else down).at[u, rows_of(which, c)]

    def line(u, c, to, sems, own=False):
        source = (up_hbm if c == chunks else down_hbm).at[rows_of(part, c)] if own else place(u, part, c)
        return pltpu.make_async_remote_copy(
            src_ref=source, dst_ref=place(u, part, c), send_sem=sems.at[u, c],
            recv_sem=line_sem.at[u, c], device_id=(part, to, mine), device_id_type=MESH)

    def pair(u, c, which):
        return pltpu.make_async_remote_copy(
            src_ref=place(u, which, c), dst_ref=place(u, which, c), send_sem=pair_send.at[u, c],
            recv_sem=pair_recv.at[u, c], device_id=(1 - part, me, mine), device_id_type=MESH)

    def send_own(c):
        for to, there, sems in ((me + 1, has_right, right_sem), (me - 1, has_left, left_sem)):
            @pl.when(there)
            def _():
                line(me, c, to, sems, own=True).start()

    first_pieces = min(window or chunks, chunks)
    for c in range(first_pieces):
        send_own(c)

    @pl.when((me == 0) | (me == n - 1))
    def _():
        send_own(chunks + 1)

    copies[0].wait()
    copies[1].wait()

    def value_copy(peer):
        return pltpu.make_async_remote_copy(
            src_ref=value_send.at[peer], dst_ref=value_recv.at[mine], send_sem=value_ssem.at[peer],
            recv_sem=value_rsem.at[mine], device_id=(part, me, peer), device_id_type=MESH)

    def value_arrival(peer):
        return pltpu.make_async_remote_copy(
            src_ref=value_send.at[peer], dst_ref=value_recv.at[peer], send_sem=value_ssem.at[peer],
            recv_sem=value_rsem.at[peer], device_id=(part, me, peer), device_id_type=MESH)

    def block_product(owner):
        columns = pl.ds(pl.multiple_of(owner * share, share), share)
        return jnp.dot(tokens[...], weight[:, columns], preferred_element_type=F32).astype(BF16)

    @pl.loop(1, width)
    def _(i):
        peer = lax.rem(mine + i, width)
        value_send[peer] = block_product(peer)
        value_copy(peer).start()

    for c in range(first_pieces, chunks):
        send_own(c)
    base[...] = block_product(mine).astype(F32)

    position = lax.broadcasted_iota(jnp.int32, (token_count, unit), 0)

    def visit(j, carry):
        start, values = carry
        row = slot_ref[named_ref[0, j]]
        mark = row * 8 + rank_ref[row]
        return start + lengths_ref[0, j], jnp.where(position >= start, mark, values)

    for copy in copies[4:]:
        copy.wait()
    code[...] = lax.fori_loop(
        0, lengths_ref.shape[1], visit, (jnp.int32(0), jnp.zeros((token_count, unit), jnp.int32)))[1]

    column = lax.broadcasted_iota(jnp.int32, (token_count, unit), 1) // rank_pad

    def at_unit(u):
        return (code[...] >> 3) == column + u * adapters_here

    def unit_shrink(u):
        product = lax.dot_general(
            tokens[...], down[u], (((1,), (1,)), ((), ())), preferred_element_type=F32)
        return jnp.where(at_unit(u), product, 0.0)

    copies[2].wait()
    wide_sum[...] = unit_shrink(me)

    def sides(step):
        return ((me - step, me - 1, me + 1, me - step >= 0, has_right, right_sem, me == step),
                (me + step, me + 1, me - 1, me + step < n, has_left, left_sem, me + step == n - 1))

    def pass_on(step, pieces):
        for c in pieces:
            for u, source, onward, there, more, sems, end in sides(step):
                @pl.when(there & end if c == chunks + 1 else there)
                def _():
                    line(u, c, source, sems).wait_recv()

                    @pl.when(more)
                    def _():
                        line(u, c, onward, sems).start()

                    if c == chunks - 1:
                        @pl.when(jnp.logical_not(end))
                        def _():
                            pair(u, c, part).start()
                    elif c <= chunks:
                        pair(u, c, part).start()

    def take(step):
        for u, source, onward, there, more, sems, end in sides(step):
            @pl.when(there)
            def _():
                for c in range(chunks - 1):
                    pair(u, c, 1 - part).wait_recv()

                @pl.when(jnp.logical_not(end))
                def _():
                    pair(u, chunks - 1, 1 - part).wait_recv()
                wide_sum[...] += unit_shrink(u)

    down_pieces = [*range(chunks), chunks + 1]
    pass_on(1, down_pieces)
    if n == 2:
        send_own(chunks)

    @pl.loop(2, n)
    def _(step):
        pass_on(step, down_pieces)

        @pl.when(step == 2)
        def _():
            send_own(chunks)

        @pl.when(step > 2)
        def _():
            pass_on(step - 2, [chunks])

        take(step - 1)

    @pl.loop(1, width)
    def _(i):
        peer = lax.rem(mine + i, width)
        value_arrival(peer).wait_recv()
        base[...] += value_recv[peer].astype(F32)

    take(n - 1)

    def selector(height, test):
        i = lax.broadcasted_iota(jnp.int32, (height, 2 * rank_pad), 0)
        j = lax.broadcasted_iota(jnp.int32, (height, 2 * rank_pad), 1)
        return jnp.where(test(i, j), 1.0, 0.0).astype(BF16)

    fold = selector(unit, lambda i, j: i % rank_pad == j % rank_pad)
    twice = jnp.dot(wide_sum[...].astype(BF16), fold, preferred_element_type=F32)
    middle = token_count // 2
    lane = lax.broadcasted_iota(jnp.int32, (middle, 2 * rank_pad), 1)
    packed = jnp.where(lane < rank_pad, twice[:middle], twice[middle:])
    shrink_send[...] = packed.astype(BF16)

    def shrink_copy(peer, slot):
        return pltpu.make_async_remote_copy(
            src_ref=shrink_send, dst_ref=shrink_recv.at[slot], send_sem=shrink_ssem.at[peer],
            recv_sem=shrink_rsem.at[slot], device_id=(part, me, peer), device_id_type=MESH)

    for i in range(1, width):
        shrink_copy(lax.rem(mine + i, width), mine).start()
    for step in range(max(1, n - 2), n):
        pass_on(step, [chunks])
    total = shrink_send[...].astype(F32)
    for i in range(1, width):
        peer = lax.rem(mine + i, width)
        shrink_copy(peer, peer).wait_recv()
        total = total + shrink_recv[peer].astype(F32)
    narrow = total.astype(BF16)
    first = selector(2 * rank_pad, lambda i, j: i == j % rank_pad)
    second = selector(2 * rank_pad, lambda i, j: i == j % rank_pad + rank_pad)
    spread = jnp.concatenate(
        [jnp.dot(narrow, first, preferred_element_type=F32),
         jnp.dot(narrow, second, preferred_element_type=F32)], axis=0)
    lane = lax.broadcasted_iota(jnp.int32, (token_count, 2 * rank_pad), 1) % rank_pad
    spread = jnp.where(lane < 16 * (code[:, : 2 * rank_pad] & 7), spread, 0.0)
    copies_of = -(-unit // (2 * rank_pad))
    tiled = jnp.concatenate([spread] * copies_of, axis=1)[:, :unit]

    copies[3].wait()

    def lift(u, total):
        @pl.when(u != me)
        def _():
            pair(u, chunks, 1 - part).wait_recv()
        chosen = jnp.where(at_unit(u), tiled, 0.0).astype(BF16)
        return total + jnp.dot(chosen, up[u], preferred_element_type=F32)

    update = lax.fori_loop(0, n, lift, jnp.zeros((token_count, share), F32))
    scale = 32.0 / (16 * (code[:, :1] & 7)).astype(F32)
    out_ref[...] = (base[...] + update * scale).astype(BF16)

    @pl.loop(0, n)
    def _(u):
        for c in range(chunks + 1):
            if not window or c >= chunks - window:
                first = c == chunks or not window

                @pl.when((u <= me if first else u == 0) & has_right)
                def _():
                    line(u, c, me + 1, right_sem).wait_send()

                @pl.when((u >= me if first else u == n - 1) & has_left)
                def _():
                    line(u, c, me - 1, left_sem).wait_send()

            @pl.when((u != me) & (u != 0) & (u != n - 1) if c == chunks - 1 else u != me)
            def _():
                pair(u, c, part).wait_send()

    @pl.when(has_right)
    def _():
        line(0, chunks + 1, me + 1, right_sem).wait_send()

    @pl.when(has_left)
    def _():
        line(n - 1, chunks + 1, me - 1, left_sem).wait_send()

    for i in range(1, width):
        peer = lax.rem(mine + i, width)
        value_copy(peer).wait_send()
        shrink_copy(peer, mine).wait_send()


def local(n, width, tokens, value_weight, down_panels, up_panels, adapter_rank, adapter_slot, seg_adapter, seg_lengths):
    token_count, depth = tokens.shape
    adapters_here, rank_pad, _ = down_panels.shape
    share = up_panels.shape[2]
    unit = adapters_here * rank_pad
    chunks, window = (3, 0) if n <= 8 else (1, 0)
    dma = pltpu.SemaphoreType.DMA
    hbm = pl.BlockSpec(memory_space=pltpu.HBM)
    return pl.pallas_call(
        functools.partial(kernel, n, width, rank_pad, adapters_here, chunks, window),
        out_shape=jax.ShapeDtypeStruct((token_count, share), BF16),
        in_specs=[hbm] * 8,
        out_specs=pl.BlockSpec(memory_space=pltpu.VMEM),
        scratch_shapes=[
            pltpu.SMEM(adapter_rank.shape, jnp.int32),
            pltpu.SMEM(adapter_slot.shape, jnp.int32),
            pltpu.SMEM(seg_adapter.shape, jnp.int32),
            pltpu.SMEM(seg_lengths.shape, jnp.int32),
            pltpu.VMEM(tokens.shape, BF16),
            pltpu.VMEM(value_weight.shape, BF16),
            pltpu.VMEM((n, unit, depth), BF16),
            pltpu.VMEM((n, unit, share), BF16),
            pltpu.VMEM((token_count, unit), jnp.int32),
            pltpu.VMEM((token_count, unit), F32),
            pltpu.VMEM((token_count, share), F32),
            pltpu.VMEM((width, token_count, share), BF16),
            pltpu.VMEM((width, token_count, share), BF16),
            pltpu.VMEM((token_count // 2, 2 * rank_pad), BF16),
            pltpu.VMEM((width, token_count // 2, 2 * rank_pad), BF16),
            dma((8,)),
            dma((n, chunks + 2)),
            dma((n, chunks + 2)),
            dma((n, chunks + 2)),
            dma((n, chunks + 2)),
            dma((n, chunks + 2)),
            dma((width,)),
            dma((width,)),
            dma((width,)),
            dma((width,)),
        ],
        compiler_params=pltpu.CompilerParams(
            collective_id=0, has_side_effects=True, vmem_limit_bytes=62 * 1024 * 1024),
    )(tokens, value_weight, down_panels.reshape(unit, depth), up_panels.reshape(unit, share),
      adapter_rank, adapter_slot, seg_adapter, seg_lengths)


def solution(mesh):
    return jax.shard_map(
        functools.partial(local, mesh.shape["dp"], mesh.shape["tensor"]),
        mesh=mesh,
        in_specs=(
            P(("parts", "dp"), "tensor"),
            P("tensor", None),
            P("dp", None, "tensor"),
            P("dp", None, "tensor"),
            P(),
            P("parts"),
            P(("parts", "dp"), None),
            P(("parts", "dp"), None),
        ),
        out_specs=P(("parts", "dp"), "tensor"),
        check_vma=False,
    )
```

```python
import functools

import jax
import jax.numpy as jnp
from jax import lax
from jax.experimental import pallas as pl
from jax.experimental.pallas import tpu as pltpu
from jax.sharding import PartitionSpec as P

MESH = pl.DeviceIdType.MESH
BF16 = jnp.bfloat16
F32 = jnp.float32


def kernel(
    n, width, rank_pad, adapters_here, chunks, window,
    tokens_hbm, weight_hbm, down_hbm, up_hbm, rank_hbm, slot_hbm, named_hbm, lengths_hbm,
    out_ref,
    rank_ref, slot_ref, named_ref, lengths_ref,
    tokens, weight, down, up, code, wide_sum, base, value_send, value_recv, shrink_send, shrink_recv,
    local_sem, right_sem, left_sem, line_sem, pair_send, pair_recv,
    value_ssem, value_rsem, shrink_ssem, shrink_rsem,
):
    part, me, mine = lax.axis_index("parts"), lax.axis_index("dp"), lax.axis_index("tensor")
    token_count = tokens.shape[0]
    unit = adapters_here * rank_pad
    half = unit // 2
    piece = half // chunks
    share = up.shape[2]
    has_left, has_right = me > 0, me < n - 1

    copies = [
        pltpu.make_async_copy(tokens_hbm, tokens, local_sem.at[0]),
        pltpu.make_async_copy(weight_hbm, weight, local_sem.at[1]),
        pltpu.make_async_copy(down_hbm, down.at[me], local_sem.at[2]),
        pltpu.make_async_copy(up_hbm, up.at[me], local_sem.at[3]),
        pltpu.make_async_copy(rank_hbm, rank_ref, local_sem.at[4]),
        pltpu.make_async_copy(slot_hbm, slot_ref, local_sem.at[5]),
        pltpu.make_async_copy(named_hbm, named_ref, local_sem.at[6]),
        pltpu.make_async_copy(lengths_hbm, lengths_ref, local_sem.at[7]),
    ]
    barrier = pltpu.get_barrier_semaphore()

    def greet(where):
        pl.semaphore_signal(barrier, inc=1, device_id=where, device_id_type=MESH)

    @pl.when(has_left)
    def _():
        greet((part, me - 1, mine))

    @pl.when(has_right)
    def _():
        greet((part, me + 1, mine))

    greet((1 - part, me, mine))
    for i in range(1, width):
        greet((part, me, lax.rem(mine + i, width)))

    inner = has_left & has_right

    @pl.when(inner)
    def _():
        pl.semaphore_wait(barrier, width + 2)

    @pl.when(jnp.logical_not(inner))
    def _():
        pl.semaphore_wait(barrier, width + 1)

    def rows_of(which, c):
        if c == chunks + 1:
            which, c = 1 - which, chunks - 1
        if c == chunks:
            return pl.ds(pl.multiple_of(which * half, half), half)
        return pl.ds(pl.multiple_of(which * half + c * piece, piece), piece)

    def place(u, which, c):
        return (up if c == chunks else down).at[u, rows_of(which, c)]

    def line(u, c, to, sems, own=False):
        source = (up_hbm if c == chunks else down_hbm).at[rows_of(part, c)] if own else place(u, part, c)
        return pltpu.make_async_remote_copy(
            src_ref=source, dst_ref=place(u, part, c), send_sem=sems.at[u, c],
            recv_sem=line_sem.at[u, c], device_id=(part, to, mine), device_id_type=MESH)

    def pair(u, c, which):
        return pltpu.make_async_remote_copy(
            src_ref=place(u, which, c), dst_ref=place(u, which, c), send_sem=pair_send.at[u, c],
            recv_sem=pair_recv.at[u, c], device_id=(1 - part, me, mine), device_id_type=MESH)

    def send_own(c):
        for to, there, sems in ((me + 1, has_right, right_sem), (me - 1, has_left, left_sem)):
            @pl.when(there)
            def _():
                line(me, c, to, sems, own=True).start()

    first_pieces = min(window or chunks, chunks)
    for c in range(first_pieces):
        send_own(c)

    @pl.when((me == 0) | (me == n - 1))
    def _():
        send_own(chunks + 1)

    for copy in copies:
        copy.start()

    copies[0].wait()
    copies[1].wait()

    def value_copy(peer):
        return pltpu.make_async_remote_copy(
            src_ref=value_send.at[peer], dst_ref=value_recv.at[mine], send_sem=value_ssem.at[peer],
            recv_sem=value_rsem.at[mine], device_id=(part, me, peer), device_id_type=MESH)

    def value_arrival(peer):
        return pltpu.make_async_remote_copy(
            src_ref=value_send.at[peer], dst_ref=value_recv.at[peer], send_sem=value_ssem.at[peer],
            recv_sem=value_rsem.at[peer], device_id=(part, me, peer), device_id_type=MESH)

    def block_product(owner):
        columns = pl.ds(pl.multiple_of(owner * share, share), share)
        return jnp.dot(tokens[...], weight[:, columns], preferred_element_type=F32).astype(BF16)

    @pl.loop(1, width)
    def _(i):
        peer = lax.rem(mine + i, width)
        value_send[peer] = block_product(peer)
        value_copy(peer).start()

    for c in range(first_pieces, chunks):
        send_own(c)
    base[...] = block_product(mine).astype(F32)

    position = lax.broadcasted_iota(jnp.int32, (token_count, unit), 0)

    def visit(j, carry):
        start, values = carry
        row = slot_ref[named_ref[0, j]]
        mark = row * 8 + rank_ref[row]
        return start + lengths_ref[0, j], jnp.where(position >= start, mark, values)

    for copy in copies[4:]:
        copy.wait()
    code[...] = lax.fori_loop(
        0, lengths_ref.shape[1], visit, (jnp.int32(0), jnp.zeros((token_count, unit), jnp.int32)))[1]

    column = lax.broadcasted_iota(jnp.int32, (token_count, unit), 1) // rank_pad

    def at_unit(u):
        return (code[...] >> 3) == column + u * adapters_here

    def unit_shrink(u):
        product = lax.dot_general(
            tokens[...], down[u], (((1,), (1,)), ((), ())), preferred_element_type=F32)
        return jnp.where(at_unit(u), product, 0.0)

    copies[2].wait()
    wide_sum[...] = unit_shrink(me)

    def sides(step):
        return ((me - step, me - 1, me + 1, me - step >= 0, has_right, right_sem, me == step),
                (me + step, me + 1, me - 1, me + step < n, has_left, left_sem, me + step == n - 1))

    def pass_on(step, pieces):
        for c in pieces:
            for u, source, onward, there, more, sems, end in sides(step):
                @pl.when(there & end if c == chunks + 1 else there)
                def _():
                    line(u, c, source, sems).wait_recv()

                    @pl.when(more)
                    def _():
                        line(u, c, onward, sems).start()

                    if c == chunks - 1:
                        @pl.when(jnp.logical_not(end))
                        def _():
                            pair(u, c, part).start()
                    elif c <= chunks:
                        pair(u, c, part).start()

    def take(step):
        for u, source, onward, there, more, sems, end in sides(step):
            @pl.when(there)
            def _():
                for c in range(chunks - 1):
                    pair(u, c, 1 - part).wait_recv()

                @pl.when(jnp.logical_not(end))
                def _():
                    pair(u, chunks - 1, 1 - part).wait_recv()
                wide_sum[...] += unit_shrink(u)

    down_pieces = [*range(chunks), chunks + 1]
    pass_on(1, down_pieces)
    if n == 2:
        send_own(chunks)

    @pl.loop(2, n)
    def _(step):
        pass_on(step, down_pieces)

        @pl.when(step == 2)
        def _():
            send_own(chunks)

        @pl.when(step > 2)
        def _():
            pass_on(step - 2, [chunks])

        take(step - 1)

    @pl.loop(1, width)
    def _(i):
        peer = lax.rem(mine + i, width)
        value_arrival(peer).wait_recv()
        base[...] += value_recv[peer].astype(F32)

    take(n - 1)

    def selector(height, test):
        i = lax.broadcasted_iota(jnp.int32, (height, 2 * rank_pad), 0)
        j = lax.broadcasted_iota(jnp.int32, (height, 2 * rank_pad), 1)
        return jnp.where(test(i, j), 1.0, 0.0).astype(BF16)

    fold = selector(unit, lambda i, j: i % rank_pad == j % rank_pad)
    twice = jnp.dot(wide_sum[...].astype(BF16), fold, preferred_element_type=F32)
    middle = token_count // 2
    lane = lax.broadcasted_iota(jnp.int32, (middle, 2 * rank_pad), 1)
    packed = jnp.where(lane < rank_pad, twice[:middle], twice[middle:])
    shrink_send[...] = packed.astype(BF16)

    def shrink_copy(peer, slot):
        return pltpu.make_async_remote_copy(
            src_ref=shrink_send, dst_ref=shrink_recv.at[slot], send_sem=shrink_ssem.at[peer],
            recv_sem=shrink_rsem.at[slot], device_id=(part, me, peer), device_id_type=MESH)

    for i in range(1, width):
        shrink_copy(lax.rem(mine + i, width), mine).start()
    for step in range(max(1, n - 2), n):
        pass_on(step, [chunks])
    total = shrink_send[...].astype(F32)
    for i in range(1, width):
        peer = lax.rem(mine + i, width)
        shrink_copy(peer, peer).wait_recv()
        total = total + shrink_recv[peer].astype(F32)
    narrow = total.astype(BF16)
    first = selector(2 * rank_pad, lambda i, j: i == j % rank_pad)
    second = selector(2 * rank_pad, lambda i, j: i == j % rank_pad + rank_pad)
    spread = jnp.concatenate(
        [jnp.dot(narrow, first, preferred_element_type=F32),
         jnp.dot(narrow, second, preferred_element_type=F32)], axis=0)
    lane = lax.broadcasted_iota(jnp.int32, (token_count, 2 * rank_pad), 1) % rank_pad
    spread = jnp.where(lane < 16 * (code[:, : 2 * rank_pad] & 7), spread, 0.0)
    copies_of = -(-unit // (2 * rank_pad))
    tiled = jnp.concatenate([spread] * copies_of, axis=1)[:, :unit]

    copies[3].wait()

    def lift(u, total):
        @pl.when(u != me)
        def _():
            pair(u, chunks, 1 - part).wait_recv()
        chosen = jnp.where(at_unit(u), tiled, 0.0).astype(BF16)
        return total + jnp.dot(chosen, up[u], preferred_element_type=F32)

    update = lax.fori_loop(0, n, lift, jnp.zeros((token_count, share), F32))
    scale = 32.0 / (16 * (code[:, :1] & 7)).astype(F32)
    out_ref[...] = (base[...] + update * scale).astype(BF16)

    @pl.loop(0, n)
    def _(u):
        for c in range(chunks + 1):
            if not window or c >= chunks - window:
                first = c == chunks or not window

                @pl.when((u <= me if first else u == 0) & has_right)
                def _():
                    line(u, c, me + 1, right_sem).wait_send()

                @pl.when((u >= me if first else u == n - 1) & has_left)
                def _():
                    line(u, c, me - 1, left_sem).wait_send()

            @pl.when((u != me) & (u != 0) & (u != n - 1) if c == chunks - 1 else u != me)
            def _():
                pair(u, c, part).wait_send()

    @pl.when(has_right)
    def _():
        line(0, chunks + 1, me + 1, right_sem).wait_send()

    @pl.when(has_left)
    def _():
        line(n - 1, chunks + 1, me - 1, left_sem).wait_send()

    for i in range(1, width):
        peer = lax.rem(mine + i, width)
        value_copy(peer).wait_send()
        shrink_copy(peer, mine).wait_send()


def local(n, width, tokens, value_weight, down_panels, up_panels, adapter_rank, adapter_slot, seg_adapter, seg_lengths):
    token_count, depth = tokens.shape
    adapters_here, rank_pad, _ = down_panels.shape
    share = up_panels.shape[2]
    unit = adapters_here * rank_pad
    chunks, window = (3, 0) if n <= 8 else (1, 0)
    dma = pltpu.SemaphoreType.DMA
    hbm = pl.BlockSpec(memory_space=pltpu.HBM)
    return pl.pallas_call(
        functools.partial(kernel, n, width, rank_pad, adapters_here, chunks, window),
        out_shape=jax.ShapeDtypeStruct((token_count, share), BF16),
        in_specs=[hbm] * 8,
        out_specs=pl.BlockSpec(memory_space=pltpu.VMEM),
        scratch_shapes=[
            pltpu.SMEM(adapter_rank.shape, jnp.int32),
            pltpu.SMEM(adapter_slot.shape, jnp.int32),
            pltpu.SMEM(seg_adapter.shape, jnp.int32),
            pltpu.SMEM(seg_lengths.shape, jnp.int32),
            pltpu.VMEM(tokens.shape, BF16),
            pltpu.VMEM(value_weight.shape, BF16),
            pltpu.VMEM((n, unit, depth), BF16),
            pltpu.VMEM((n, unit, share), BF16),
            pltpu.VMEM((token_count, unit), jnp.int32),
            pltpu.VMEM((token_count, unit), F32),
            pltpu.VMEM((token_count, share), F32),
            pltpu.VMEM((width, token_count, share), BF16),
            pltpu.VMEM((width, token_count, share), BF16),
            pltpu.VMEM((token_count // 2, 2 * rank_pad), BF16),
            pltpu.VMEM((width, token_count // 2, 2 * rank_pad), BF16),
            dma((8,)),
            dma((n, chunks + 2)),
            dma((n, chunks + 2)),
            dma((n, chunks + 2)),
            dma((n, chunks + 2)),
            dma((n, chunks + 2)),
            dma((width,)),
            dma((width,)),
            dma((width,)),
            dma((width,)),
        ],
        compiler_params=pltpu.CompilerParams(
            collective_id=0, has_side_effects=True, vmem_limit_bytes=62 * 1024 * 1024),
    )(tokens, value_weight, down_panels.reshape(unit, depth), up_panels.reshape(unit, share),
      adapter_rank, adapter_slot, seg_adapter, seg_lengths)


def solution(mesh):
    return jax.shard_map(
        functools.partial(local, mesh.shape["dp"], mesh.shape["tensor"]),
        mesh=mesh,
        in_specs=(
            P(("parts", "dp"), "tensor"),
            P("tensor", None),
            P("dp", None, "tensor"),
            P("dp", None, "tensor"),
            P(),
            P("parts"),
            P(("parts", "dp"), None),
            P(("parts", "dp"), None),
        ),
        out_specs=P(("parts", "dp"), "tensor"),
        check_vma=False,
    )
```
